256 devices in a mesh: tm: 8 (over z_hi, core), gz: 32 (over z_lo, x, y).
Axes of the slice: x: 4, y: 4, z: 8 (z_hi: 4, z_lo: 2; z = z_hi * 2 + z_lo), core: 2. Of those that a mesh axis runs over, the one named last changes fastest.
Arguments:
- start_states: float32 [8, 256, 64, 256], P('tm', 'gz'), may hold values from -1.2 to 1.2
Outputs:
- new_states: float32 [8, 256, 64, 256], P('tm', 'gz')
The draws below stay inside these ranges and needn't reach their ends.
All inputs are finite; a program needn't handle non-finite values.
Results may differ from the reference program's by a relative error of at most 0.000086.
Values sent between devices are 32-bit elements; how exact they have to be, the bound alone decides.
No kernel may reach another device: no remote copies, remote signals or barrier semaphores. Data moves between devices by JAX's collectives and lax.ppermute only.
A program may use at most 64 MiB of HBM per device.

```python
import math
import jax
import jax.numpy as jnp
from jax import lax

CZ = 8
NX = 64
NY = 256
COARSE_STEPS = 2
FINE_STEPS = 8
SLABS = 8
NZ = 256


def draw_start_states(key, part):
    key = jax.random.fold_in(key, 7)
    keys = jax.random.split(key, 3)
    phases = jax.random.uniform(keys[0], (3, SLABS, 1, 1, 1), jnp.float32, 0.0, 2.0 * math.pi)
    stretch = jax.random.uniform(keys[1], (SLABS, 1, 1, 1), jnp.float32, 0.8, 1.25)
    rough = jax.random.uniform(keys[2], (SLABS, NZ, NX, NY), jnp.float32, -1.0, 1.0)
    zpos = jnp.arange(NZ, dtype=jnp.float32)[None, :, None, None]
    xpos = jnp.arange(NX, dtype=jnp.float32)[None, None, :, None]
    ypos = jnp.arange(NY, dtype=jnp.float32)[None, None, None, :]
    along_z = jnp.sin(zpos * stretch * (2.0 * math.pi / (3.0 * CZ)) + phases[0])
    across = jnp.sin(xpos * (2.0 * math.pi / NX) + phases[1]) * jnp.sin(ypos * (4.0 * math.pi / NY) + phases[2])
    level = 0.95
    spread = 0.25
    smooth = jnp.tanh(2.5 * (along_z + 0.6 * across))
    return level * smooth + spread * rough


def setup_inputs(seed: int = 0) -> dict:
    key_of = jax.random.split(jax.random.key(seed), 2)
    return {
        "start_states": draw_start_states(jax.random.fold_in(key_of[1], 71), 0),
    }


fine_dt = 0.025
coarse_dt = 0.1
fine_coef = 4.8
coarse_coef = 1.2


def rate(padded, coef):
    center = padded[1:-1]
    lap = padded[2:] + padded[:-2]
    lap = lap + jnp.roll(center, 1, 1) + jnp.roll(center, -1, 1)
    lap = lap + jnp.roll(center, 1, 2) + jnp.roll(center, -1, 2)
    lap = lap - 6.0 * center
    return coef * lap + center - center * center * center


def zero_pad(field):
    return jnp.pad(field, ((1, 1), (0, 0), (0, 0)))


def heun(field, coef, step_size):
    first = rate(zero_pad(field), coef)
    middle = field + step_size * first
    second = rate(zero_pad(middle), coef)
    return field + (0.5 * step_size) * (first + second)


def fine_propagate(field):
    for step in range(FINE_STEPS):
        field = heun(field, fine_coef, fine_dt)
    return field


def coarse_propagate(field):
    for step in range(COARSE_STEPS):
        field = heun(field, coarse_coef, coarse_dt)
    return field


def restrict(field):
    field = field[0::2] + field[1::2]
    field = field[:, 0::2] + field[:, 1::2]
    field = field[:, :, 0::2] + field[:, :, 1::2]
    return field * 0.125


def prolong(field):
    return jnp.repeat(jnp.repeat(jnp.repeat(field, 2, 0), 2, 1), 2, 2)


def reference(start_states):
    slabs = start_states.shape[0]
    fine_end = lax.map(fine_propagate, start_states)
    coarse_start = lax.map(restrict, start_states)
    coarse_old = lax.map(coarse_propagate, coarse_start)
    jumps = lax.map(restrict, fine_end) - coarse_old
    current = coarse_start[0]
    results = []
    for slab in range(slabs):
        advanced = coarse_propagate(current)
        results.append(prolong(advanced) + (fine_end[slab] - prolong(coarse_old[slab])))
        current = advanced + jumps[slab]
    return jnp.stack(results)
```

```python
import functools
import math

import jax
import jax.numpy as jnp
from jax import lax
from jax.experimental import pallas as pl
from jax.experimental.pallas import tpu as pltpu
from jax.sharding import PartitionSpec as P

COARSE_STEPS = 2
FINE_STEPS = 8

fine_dt = 0.025
coarse_dt = 0.1
fine_coef = 4.8
coarse_coef = 1.2

KAPPA = math.sqrt(fine_dt)
FINE_A = 1.0 + fine_dt * (1.0 - 6.0 * fine_coef)
FINE_C = fine_dt * fine_coef
COARSE_A = 1.0 + coarse_dt * (1.0 - 6.0 * coarse_coef)
COARSE_B = coarse_dt / fine_dt
COARSE_C = coarse_dt * coarse_coef

CZ, NX, NY = 8, 64, 256
WIDE = 2 * FINE_STEPS
CC, CX, CY = CZ // 2, NX // 2, NY // 2
REACH = 2 * COARSE_STEPS
VMEM_LIMIT = 40 * 1024 * 1024


def x_sum(a):
    n = a.shape[0]
    after = jnp.concatenate([a[8:], pltpu.roll(a[:8], 7, 0)], axis=0)
    before = jnp.concatenate([pltpu.roll(a[n - 8 :], 1, 0), a[: n - 8]], axis=0)
    return after + before


def split_dot(a, m):
    hi = a.astype(jnp.bfloat16)
    rest = a - hi.astype(jnp.float32)
    mid = rest.astype(jnp.bfloat16)
    low = (rest - mid.astype(jnp.float32)).astype(jnp.bfloat16)
    dot = functools.partial(jnp.dot, preferred_element_type=jnp.float32)
    return dot(hi, m) + (dot(mid, m) + dot(low, m))


def fine_euler(src, p, c):
    out = []
    for j, by in ((0, 1), (1, CY - 1)):
        a = src[p, j]
        b = src[p, 1 - j]
        total = (src[p - 1, j] + src[p + 1, j]) + (x_sum(a) + (b + pltpu.roll(b, by, 1)))
        out.append(c * total + a * (FINE_A - a * a))
    return out


def coarse_euler(src, p, c):
    a = src[p]
    total = (src[p - 1] + src[p + 1]) + (x_sum(a) + (pltpu.roll(a, 1, 1) + pltpu.roll(a, CY - 1, 1)))
    return c * total + a * (COARSE_A - COARSE_B * (a * a))


def inside(first, p, count, coef):
    g = first + p
    return jnp.where((g >= 0) & (g < count), coef, 0.0).astype(jnp.float32)


def coarse_propagate(v, v1, first, count):
    n = CC + 2 * REACH
    for step in range(COARSE_STEPS):
        lo = 2 * step + 1
        for p in range(lo, n - lo):
            v1[p] = coarse_euler(v, p, inside(first, p, count, COARSE_C))
        for p in range(lo + 1, n - lo - 1):
            v[p] = 0.5 * (v[p] + coarse_euler(v1, p, inside(first, p, count, COARSE_C)))


def restricted(v, p):
    s = (v[p, 0] + v[p + 1, 0]) + (v[p, 1] + v[p + 1, 1])
    rows = [s[16 * i : 16 * i + 8] + s[16 * i + 8 : 16 * i + 16] for i in range(4)]
    return 0.125 * jnp.concatenate(rows, axis=0)


def prep_kernel(x_ref, out_ref, x, sems):
    copies = []
    for h in range(2):
        copies.append(pltpu.make_async_copy(x_ref.at[0, :, :, pl.ds(h * CY, CY)], x.at[h], sems.at[h]))
        copies[-1].start()
    y = lax.broadcasted_iota(jnp.int32, (NY, NY), 0)
    k = lax.broadcasted_iota(jnp.int32, (NY, NY), 1)
    m = (y == 2 * (k % CY) + k // CY).astype(jnp.float32).astype(jnp.bfloat16)

    for copy in copies:
        copy.wait()

    def body(p, carry):
        halves = []
        for h in range(2):
            rows = [x[h, p, pl.ds(i, 8, stride=8), :] for i in range(8)]
            halves.append(jnp.concatenate(rows, axis=0))
        r = split_dot(jnp.concatenate(halves, axis=1), m) * KAPPA
        out_ref[p, 0] = r[:, :CY]
        out_ref[p, 1] = r[:, CY:]
        return carry

    lax.fori_loop(0, CZ, body, 0)


def fine_kernel(
    blocks, place_ref, l2, l1, own, r1, r2, fe_ref, co_ref, jump_ref, send_ref, v, v1, cv, cv1, sems
):
    place = place_ref[0]
    copies = []
    for n, ref in enumerate((l2, l1, own, r1, r2)):
        copies.append(pltpu.make_async_copy(ref, v.at[pl.ds(n * CZ, CZ)], sems.at[n]))
        copies[-1].start()
    for copy in copies:
        copy.wait()
    for q in range(CC + 2 * REACH):
        cv[q] = restricted(v, WIDE - 2 * REACH + 2 * q)
    coarse_propagate(cv, cv1, place * CC - REACH, blocks * CC)
    first = place * CZ - WIDE
    n = CZ + 2 * WIDE
    for step in range(FINE_STEPS):
        lo = 2 * step + 1

        def predict(p, carry):
            a, b = fine_euler(v, p, inside(first, p, blocks * CZ, FINE_C))
            v1[p, 0] = a
            v1[p, 1] = b
            return carry

        def correct(p, carry):
            a, b = fine_euler(v1, p, inside(first, p, blocks * CZ, FINE_C))
            v[p, 0] = 0.5 * (v[p, 0] + a)
            v[p, 1] = 0.5 * (v[p, 1] + b)
            return carry

        lax.fori_loop(lo, n - lo, predict, 0)
        lax.fori_loop(lo + 1, n - lo - 1, correct, 0)
    fe_ref[...] = v[pl.ds(WIDE, CZ)]
    for q in range(CC):
        old = cv[REACH + q]
        jump = restricted(v, WIDE + 2 * q) - old
        co_ref[q] = old
        jump_ref[q] = jump
        send_ref[q] = old + jump


def sweep_kernel(blocks, turn, place_ref, left, mid, right, jump_ref, picked_ref, out_ref, send_ref, cv, cv1):
    place = place_ref[0]
    slab = place_ref[1]

    @pl.when(slab == turn)
    def _():
        for n, ref in enumerate((left, mid, right)):
            cv[pl.ds(n * CC, CC)] = ref[...]
        coarse_propagate(cv, cv1, place * CC - REACH, blocks * CC)
        for q in range(CC):
            new = cv[REACH + q]
            out_ref[q] = new
            send_ref[q] = new + jump_ref[q]

    @pl.when(slab != turn)
    def _():
        out_ref[...] = picked_ref[...]
        send_ref[...] = jump_ref[...]


def final_kernel(fe_ref, co_ref, picked_ref, out_ref, x, sems):
    k = lax.broadcasted_iota(jnp.int32, (NY, NY), 0)
    y = lax.broadcasted_iota(jnp.int32, (NY, NY), 1)
    m = (y == 2 * (k % CY) + k // CY).astype(jnp.float32).astype(jnp.bfloat16)

    def body(p, carry):
        new = picked_ref[p // 2]
        old = co_ref[p // 2]

        def spread(a):
            rows = []
            for i in range(8):
                rows.append(a[8 * (i // 2) : 8 * (i // 2) + 8])
            return jnp.concatenate(rows, axis=0)

        new = spread(new)
        old = spread(old)
        r = jnp.concatenate([new + (fe_ref[p, j] - old) for j in range(2)], axis=1)
        r = split_dot(r, m) * (1.0 / KAPPA)
        for h in range(2):
            for i in range(8):
                x[h, p, pl.ds(i, 8, stride=8), :] = r[8 * i : 8 * i + 8, h * CY : (h + 1) * CY]
        return carry

    lax.fori_loop(0, CZ, body, 0)
    copies = []
    for h in range(2):
        copies.append(pltpu.make_async_copy(x.at[h], out_ref.at[0, :, :, pl.ds(h * CY, CY)], sems.at[h]))
        copies[-1].start()
    for copy in copies:
        copy.wait()


VM = pl.BlockSpec(memory_space=pltpu.VMEM)
SM = pl.BlockSpec(memory_space=pltpu.SMEM)
HB = pl.BlockSpec(memory_space=pl.ANY)
PARAMS = pltpu.CompilerParams(vmem_limit_bytes=VMEM_LIMIT)
fine_shape = jax.ShapeDtypeStruct((CZ, 2, NX, CY), jnp.float32)
coarse_shape = jax.ShapeDtypeStruct((CC, CX, CY), jnp.float32)
HALVES = [pltpu.VMEM((2, CZ, NX, CY), jnp.float32), pltpu.SemaphoreType.DMA((2,))]


def shifted(array, by):
    count = lax.axis_size("gz")
    return lax.ppermute(array, "gz", [(i, i + by) for i in range(count) if 0 <= i + by < count])


def handed(array, turn, by):
    count = lax.axis_size("gz")
    pairs = [((turn - 1) * count + i, turn * count + i + by) for i in range(count) if 0 <= i + by < count]
    return lax.ppermute(array, ("tm", "gz"), pairs)


def per_device(start_states):
    blocks = lax.axis_size("gz")
    slabs = lax.axis_size("tm")
    place = jnp.stack([lax.axis_index("gz"), lax.axis_index("tm")]).astype(jnp.int32)
    own = pl.pallas_call(
        prep_kernel,
        out_shape=fine_shape,
        in_specs=[HB],
        out_specs=VM,
        scratch_shapes=HALVES,
        compiler_params=PARAMS,
    )(start_states)
    l1, r1, l2, r2 = shifted(own, 1), shifted(own, -1), shifted(own, 2), shifted(own, -2)
    wide = (CZ + 2 * WIDE, 2, NX, CY)
    coarse_wide = (CC + 2 * REACH, CX, CY)
    fine_end, coarse_old, jump, send = pl.pallas_call(
        functools.partial(fine_kernel, blocks),
        out_shape=(fine_shape, coarse_shape, coarse_shape, coarse_shape),
        in_specs=[SM] + [HB] * 5,
        out_specs=(VM,) * 4,
        scratch_shapes=[
            pltpu.VMEM(wide, jnp.float32),
            pltpu.VMEM(wide, jnp.float32),
            pltpu.VMEM(coarse_wide, jnp.float32),
            pltpu.VMEM(coarse_wide, jnp.float32),
            pltpu.SemaphoreType.DMA((5,)),
        ],
        compiler_params=PARAMS,
    )(place, l2, l1, own, r1, r2)
    picked = coarse_old
    for turn in range(1, slabs):
        left, mid, right = handed(send, turn, 1), handed(send, turn, 0), handed(send, turn, -1)
        picked, send = pl.pallas_call(
            functools.partial(sweep_kernel, blocks, turn),
            out_shape=(coarse_shape, coarse_shape),
            in_specs=[SM] + [VM] * 5,
            out_specs=(VM,) * 2,
            scratch_shapes=[pltpu.VMEM(coarse_wide, jnp.float32)] * 2,
            compiler_params=PARAMS,
        )(place, left, mid, right, jump, picked)
    return pl.pallas_call(
        final_kernel,
        out_shape=jax.ShapeDtypeStruct((1, CZ, NX, NY), jnp.float32),
        in_specs=[VM] * 3,
        out_specs=HB,
        scratch_shapes=HALVES,
        compiler_params=PARAMS,
    )(fine_end, coarse_old, picked)


def solution(mesh):
    placed = (P("tm", "gz", None, None),)
    return jax.shard_map(
        per_device, mesh=mesh, in_specs=placed, out_specs=P("tm", "gz", None, None), check_vma=False
    )
```

```python
import functools
import math

import jax
import jax.numpy as jnp
from jax import lax
from jax.experimental import pallas as pl
from jax.experimental.pallas import tpu as pltpu
from jax.sharding import PartitionSpec as P

COARSE_STEPS = 2
FINE_STEPS = 8

fine_dt = 0.025
coarse_dt = 0.1
fine_coef = 4.8
coarse_coef = 1.2

KAPPA = math.sqrt(fine_dt)
FINE_A = 1.0 + fine_dt * (1.0 - 6.0 * fine_coef)
FINE_C = fine_dt * fine_coef
COARSE_A = 1.0 + coarse_dt * (1.0 - 6.0 * coarse_coef)
COARSE_B = coarse_dt / fine_dt
COARSE_C = coarse_dt * coarse_coef

CZ, NX, NY = 8, 64, 256
ROUNDS = 2
WIDE = 2 * FINE_STEPS // ROUNDS
CC, CX, CY = CZ // 2, NX // 2, NY // 2
REACH = 2 * COARSE_STEPS
VMEM_LIMIT = 40 * 1024 * 1024


def x_sum(a):
    n = a.shape[0]
    after = jnp.concatenate([a[8:], pltpu.roll(a[:8], 7, 0)], axis=0)
    before = jnp.concatenate([pltpu.roll(a[n - 8 :], 1, 0), a[: n - 8]], axis=0)
    return after + before


def split_dot(a, m):
    hi = a.astype(jnp.bfloat16)
    rest = a - hi.astype(jnp.float32)
    mid = rest.astype(jnp.bfloat16)
    low = (rest - mid.astype(jnp.float32)).astype(jnp.bfloat16)
    dot = functools.partial(jnp.dot, preferred_element_type=jnp.float32)
    return dot(hi, m) + (dot(mid, m) + dot(low, m))


def fine_euler(get, p, c):
    out = []
    for j, by in ((0, 1), (1, CY - 1)):
        a = get(p, j)
        b = get(p, 1 - j)
        total = (get(p - 1, j) + get(p + 1, j)) + (x_sum(a) + (b + pltpu.roll(b, by, 1)))
        out.append(c * total + a * (FINE_A - a * a))
    return out


def coarse_euler(get, p, c):
    a = get(p)
    total = (get(p - 1) + get(p + 1)) + (x_sum(a) + (pltpu.roll(a, 1, 1) + pltpu.roll(a, CY - 1, 1)))
    return c * total + a * (COARSE_A - COARSE_B * (a * a))


def inside(first, p, count, coef):
    g = first + p
    return jnp.where((g >= 0) & (g < count), coef, 0.0).astype(jnp.float32)


def coarse_propagate(get, v, v1, lo, hi, first, count):
    for step in range(COARSE_STEPS):
        lo, hi = lo + 1, hi - 1
        for p in range(lo, hi):
            v1[p] = coarse_euler(get, p, inside(first, p, count, COARSE_C))
        lo, hi = lo + 1, hi - 1
        for p in range(lo, hi):
            new = coarse_euler(lambda q: v1[q], p, inside(first, p, count, COARSE_C))
            v[p] = 0.5 * (get(p) + new)
        get = lambda q: v[q]


def restricted(get, p):
    s = (get(p, 0) + get(p + 1, 0)) + (get(p, 1) + get(p + 1, 1))
    rows = [s[16 * i : 16 * i + 8] + s[16 * i + 8 : 16 * i + 16] for i in range(4)]
    return 0.125 * jnp.concatenate(rows, axis=0)


def prep_kernel(x_ref, out_ref, x, sems):
    copies = [pltpu.make_async_copy(x_ref.at[0, p], x.at[p], sems.at[p]) for p in range(CZ)]
    for copy in copies:
        copy.start()
    y = lax.broadcasted_iota(jnp.int32, (NY, NY), 0)
    k = lax.broadcasted_iota(jnp.int32, (NY, NY), 1)
    m = (y == 2 * (k % CY) + k // CY).astype(jnp.float32).astype(jnp.bfloat16)
    for p in range(CZ):
        copies[p].wait()
        r = split_dot(x[p], m) * KAPPA
        for s in range(8):
            for j in range(2):
                out_ref[p, j, pl.ds(s, 8, stride=8), :] = r[8 * s : 8 * s + 8, j * CY : (j + 1) * CY]


def three(left, mid, right, n):
    def get(p, *rest):
        ref = (left, mid, right)[p // n]
        return ref[(p % n,) + rest]

    return get


def sides(place, n):
    at = jnp.where(place % 2 == 1, 2 * n, 0)
    return at, 2 * n - at


def fine_rounds(own, one, two, put, v, v1, place, blocks):
    for at, ref in zip(sides(place, CZ), (one, two)):
        for p in range(CZ):
            v[at + p] = ref[p]
    get = lambda q, j: own[q - CZ, j] if CZ <= q < 2 * CZ else v[q, j]
    first = place * CZ - WIDE
    n = CZ + 2 * WIDE
    for step in range(WIDE // 2):
        lo = 2 * step + 1
        for p in range(lo, n - lo):
            a, b = fine_euler(get, p, inside(first, p, blocks * CZ, FINE_C))
            v1[p, 0] = a
            v1[p, 1] = b
        for p in range(lo + 1, n - lo - 1):
            a, b = fine_euler(lambda q, j: v1[q, j], p, inside(first, p, blocks * CZ, FINE_C))
            a = 0.5 * (get(p, 0) + a)
            b = 0.5 * (get(p, 1) + b)
            if lo + 1 == WIDE:
                put(p - WIDE, a, b)
            else:
                v[p, 0] = a
                v[p, 1] = b
        get = lambda q, j: v[q, j]


def fine_kernel(blocks, place_ref, own, two, one, out_ref, v, v1):
    def put(p, a, b):
        out_ref[p, 0] = a
        out_ref[p, 1] = b

    fine_rounds(own, one, two, put, v, v1, place_ref[0], blocks)


def last_fine_kernel(blocks, place_ref, own, two, one, co_ref, out_ref, jump_ref, send_ref, v, v1):
    def put(p, a, b):
        out_ref[p, 0] = a
        out_ref[p, 1] = b

    fine_rounds(own, one, two, put, v, v1, place_ref[0], blocks)
    for q in range(CC):
        old = co_ref[q]
        jump = restricted(lambda p, j: out_ref[p, j], 2 * q) - old
        jump_ref[q] = jump
        send_ref[q] = jnp.where(place_ref[1] == 0, old + jump, jump)


def coarse_kernel(blocks, place_ref, own, two, one, co_ref, cv, cv1):
    at, then = sides(place_ref[0], CC)
    for ref, base in ((own, CC), (one, at), (two, then)):
        for q in range(CC):
            cv[base + q] = restricted(lambda p, j: ref[p, j], 2 * q)
    first = (place_ref[0] - 1) * CC
    coarse_propagate(lambda q: cv[q], cv, cv1, 0, 3 * CC, first, blocks * CC)
    for q in range(CC):
        co_ref[q] = cv[CC + q]


def first_sweep_kernel(blocks, place_ref, left, mid, right, jump_ref, old_ref, out_ref, send_ref, cv, cv1):
    @pl.when(place_ref[1] == 1)
    def _():
        first = (place_ref[0] - 1) * CC
        coarse_propagate(three(left, mid, right, CC), cv, cv1, 0, 3 * CC, first, blocks * CC)
        for q in range(CC):
            new = cv[CC + q]
            out_ref[q] = new
            send_ref[q] = new + jump_ref[q]

    @pl.when(place_ref[1] != 1)
    def _():
        out_ref[...] = old_ref[...]
        send_ref[...] = jump_ref[...]


def sweep_kernel(
    blocks, slab, place_ref, a0, a1, a2, a3, a4, j0, j1, j2, jump_ref, old_ref, oldx_ref,
    out_ref, outx_ref, send_ref, cv, cv1,
):
    @pl.when(place_ref[1] == slab)
    def _():
        refs = (a0, a1, a2, a3, a4)
        first = (place_ref[0] - 2) * CC
        get = lambda p: refs[p // CC][p % CC]
        coarse_propagate(get, cv, cv1, 0, 5 * CC, first, blocks * CC)
        for q in range(CC):
            outx_ref[q] = cv[2 * CC + q]
        wide = three(j0, j1, j2, CC)
        for q in range(CC, 4 * CC):
            cv[q] = cv[q] + wide(q - CC)
        coarse_propagate(lambda q: cv[q], cv, cv1, CC, 4 * CC, first, blocks * CC)
        for q in range(CC):
            new = cv[2 * CC + q]
            out_ref[q] = new
            send_ref[q] = new + jump_ref[q]

    @pl.when(place_ref[1] != slab)
    def _():
        out_ref[...] = old_ref[...]
        outx_ref[...] = oldx_ref[...]
        send_ref[...] = jump_ref[...]


def interleave():
    k = lax.broadcasted_iota(jnp.int32, (NY, NY), 0)
    y = lax.broadcasted_iota(jnp.int32, (NY, NY), 1)
    return (y == 2 * (k % CY) + k // CY).astype(jnp.float32).astype(jnp.bfloat16)


def spread(a):
    return jnp.concatenate([a[8 * (i // 2) : 8 * (i // 2) + 8] for i in range(8)], axis=0)


def rest_kernel(fe_ref, co_ref, out_ref):
    m = interleave()
    for p in range(CZ):
        old = spread(co_ref[p // 2])
        r = jnp.concatenate([fe_ref[p, j] - old for j in range(2)], axis=1)
        r = split_dot(r, m) * (1.0 / KAPPA)
        for h in range(2):
            for i in range(8):
                out_ref[h, p, pl.ds(i, 8, stride=8), :] = r[8 * i : 8 * i + 8, h * CY : (h + 1) * CY]


def final_kernel(place_ref, rest_ref, picked_ref, even_ref, out_ref, x, sems):
    slab = place_ref[1]
    use_even = (slab % 2 == 0) & (slab > 0)
    k = lax.broadcasted_iota(jnp.int32, (CY, NY), 0)
    y = lax.broadcasted_iota(jnp.int32, (CY, NY), 1)
    m = (k == y // 2).astype(jnp.float32).astype(jnp.bfloat16)
    copies = []
    for q in range(CC):
        new = jnp.where(use_even, even_ref[q], picked_ref[q])
        r = split_dot(new, m) * (1.0 / KAPPA)
        for p in (2 * q, 2 * q + 1):
            for h in range(2):
                for i in range(8):
                    at = (h, p, pl.ds(i, 8, stride=8), slice(None))
                    c = 8 * (i // 2)
                    x[at] = rest_ref[at] + r[c : c + 8, h * CY : (h + 1) * CY]
                dst = out_ref.at[0, p, :, pl.ds(h * CY, CY)]
                copies.append(pltpu.make_async_copy(x.at[h, p], dst, sems.at[p, h]))
                copies[-1].start()
    for copy in copies:
        copy.wait()


VM = pl.BlockSpec(memory_space=pltpu.VMEM)
SM = pl.BlockSpec(memory_space=pltpu.SMEM)
HB = pl.BlockSpec(memory_space=pltpu.HBM)
PARAMS = pltpu.CompilerParams(vmem_limit_bytes=VMEM_LIMIT)
fine_shape = jax.ShapeDtypeStruct((CZ, 2, NX, CY), jnp.float32)
half_shape = jax.ShapeDtypeStruct((2, CZ, NX, CY), jnp.float32)
coarse_shape = jax.ShapeDtypeStruct((CC, CX, CY), jnp.float32)
WHOLE = [pltpu.VMEM((CZ, NX, NY), jnp.float32), pltpu.SemaphoreType.DMA((CZ,))]
HALVES = [pltpu.VMEM((2, CZ, NX, CY), jnp.float32), pltpu.SemaphoreType.DMA((CZ, 2))]
FINE_WORK = [pltpu.VMEM((CZ + 2 * WIDE, 2, NX, CY), jnp.float32)] * 2


def coarse_work(n):
    return [pltpu.VMEM((n * CC, CX, CY), jnp.float32)] * 2


def call(kernel, out_shape, in_specs, args, scratch=(), out_specs=None):
    if out_specs is None:
        out_specs = (VM,) * len(out_shape) if isinstance(out_shape, tuple) else VM
    return pl.pallas_call(
        kernel,
        out_shape=out_shape,
        in_specs=in_specs,
        out_specs=out_specs,
        scratch_shapes=list(scratch),
        compiler_params=PARAMS,
    )(*args)


def both(array):
    count = lax.axis_size("gz")
    pairs = [[(i, i + 1) for i in range(edge, count - 1, 2)] for edge in (1, 0)]
    one, two = (lax.ppermute(array, "gz", p + [(j, i) for i, j in p]) for p in pairs)
    return two, one


def handed(array, slabs, by=0):
    count = lax.axis_size("gz")
    pairs = [(a * count + i, b * count + i + by) for a, b in slabs for i in range(count) if 0 <= i + by < count]
    return lax.ppermute(array, ("tm", "gz"), pairs)


def per_device(start_states):
    blocks = lax.axis_size("gz")
    slabs = lax.axis_size("tm")
    place = jnp.stack([lax.axis_index("gz"), lax.axis_index("tm")]).astype(jnp.int32)
    start_states = pltpu.with_memory_space_constraint(start_states, pltpu.HBM)
    own = call(prep_kernel, fine_shape, [HB], (start_states,), WHOLE)
    near = (place, own, *both(own))
    own = call(functools.partial(fine_kernel, blocks), fine_shape, [SM] + [VM] * 3, near, FINE_WORK)
    two, one = both(own)
    old = call(functools.partial(coarse_kernel, blocks), coarse_shape, [SM] + [VM] * 3, near, coarse_work(3))
    fine_end, jump, send = call(
        functools.partial(last_fine_kernel, blocks),
        (fine_shape, coarse_shape, coarse_shape),
        [SM] + [VM] * 4,
        (place, own, two, one, old),
        FINE_WORK,
    )
    firsts = range(0, slabs - 1, 2)
    side = [handed(send, [(k, k + 1) for k in firsts], by) for by in (1, 0, -1)]
    picked, send = call(
        functools.partial(first_sweep_kernel, blocks),
        (coarse_shape,) * 2,
        [SM] + [VM] * 5,
        (place, *side, jump, old),
        coarse_work(3),
    )
    rest = call(rest_kernel, half_shape, [VM] * 2, (fine_end, old))
    even = jump
    for k in firsts[1:]:
        got = [handed(send, [(k - 1, k + 1)], by) for by in (2, 1, 0, -1, -2)]
        picked, even, send = call(
            functools.partial(sweep_kernel, blocks, k + 1),
            (coarse_shape,) * 3,
            [SM] + [VM] * 11,
            (place, *got, *side, jump, picked, even),
            coarse_work(5),
        )
    even = handed(even, [(k + 1, k) for k in firsts[1:]])
    return call(
        final_kernel,
        jax.ShapeDtypeStruct((1, CZ, NX, NY), jnp.float32),
        [SM] + [VM] * 3,
        (place, rest, picked, even),
        HALVES,
        HB,
    )


def solution(mesh):
    placed = (P("tm", "gz", None, None),)
    return jax.shard_map(
        per_device, mesh=mesh, in_specs=placed, out_specs=P("tm", "gz", None, None), check_vma=False
    )
```

```python
import functools
import math

import jax
import jax.numpy as jnp
from jax import lax
from jax.experimental import pallas as pl
from jax.experimental.pallas import tpu as pltpu
from jax.sharding import PartitionSpec as P

COARSE_STEPS = 2
FINE_STEPS = 8

fine_dt = 0.025
coarse_dt = 0.1
fine_coef = 4.8
coarse_coef = 1.2

KAPPA = math.sqrt(fine_dt)
FINE_A = 1.0 + fine_dt * (1.0 - 6.0 * fine_coef)
FINE_C = fine_dt * fine_coef
COARSE_A = 1.0 + coarse_dt * (1.0 - 6.0 * coarse_coef)
COARSE_B = coarse_dt / fine_dt
COARSE_C = coarse_dt * coarse_coef

CZ, NX, NY = 8, 64, 256
ROUNDS = 2
WIDE = 2 * FINE_STEPS // ROUNDS
CC, CX, CY = CZ // 2, NX // 2, NY // 2
REACH = 2 * COARSE_STEPS
VMEM_LIMIT = 40 * 1024 * 1024


def x_sum(a):
    n = a.shape[0]
    after = jnp.concatenate([a[8:], pltpu.roll(a[:8], 7, 0)], axis=0)
    before = jnp.concatenate([pltpu.roll(a[n - 8 :], 1, 0), a[: n - 8]], axis=0)
    return after + before


def split_dot(a, m):
    hi = a.astype(jnp.bfloat16)
    rest = a - hi.astype(jnp.float32)
    mid = rest.astype(jnp.bfloat16)
    low = (rest - mid.astype(jnp.float32)).astype(jnp.bfloat16)
    dot = functools.partial(jnp.dot, preferred_element_type=jnp.float32)
    return dot(hi, m) + (dot(mid, m) + dot(low, m))


def fine_euler(get, p, c):
    out = []
    for j, by in ((0, 1), (1, CY - 1)):
        a = get(p, j)
        b = get(p, 1 - j)
        total = (get(p - 1, j) + get(p + 1, j)) + (x_sum(a) + (b + pltpu.roll(b, by, 1)))
        out.append(c * total + a * (FINE_A - a * a))
    return out


def coarse_euler(get, p, c):
    a = get(p)
    total = (get(p - 1) + get(p + 1)) + (x_sum(a) + (pltpu.roll(a, 1, 1) + pltpu.roll(a, CY - 1, 1)))
    return c * total + a * (COARSE_A - COARSE_B * (a * a))


def inside(first, p, count, coef):
    g = first + p
    return jnp.where((g >= 0) & (g < count), coef, 0.0).astype(jnp.float32)


def coarse_propagate(get, v, v1, lo, hi, first, count):
    for step in range(COARSE_STEPS):
        lo, hi = lo + 1, hi - 1
        for p in range(lo, hi):
            v1[p] = coarse_euler(get, p, inside(first, p, count, COARSE_C))
        lo, hi = lo + 1, hi - 1
        for p in range(lo, hi):
            new = coarse_euler(lambda q: v1[q], p, inside(first, p, count, COARSE_C))
            v[p] = 0.5 * (get(p) + new)
        get = lambda q: v[q]


def restricted(get, p):
    s = (get(p, 0) + get(p + 1, 0)) + (get(p, 1) + get(p + 1, 1))
    rows = [s[16 * i : 16 * i + 8] + s[16 * i + 8 : 16 * i + 16] for i in range(4)]
    return 0.125 * jnp.concatenate(rows, axis=0)


def prep_kernel(x_ref, even_ref, odd_ref, x, sems):
    copies = [pltpu.make_async_copy(x_ref.at[0, p], x.at[p], sems.at[p]) for p in range(CZ)]
    for copy in copies:
        copy.start()
    y = lax.broadcasted_iota(jnp.int32, (NY, NY), 0)
    k = lax.broadcasted_iota(jnp.int32, (NY, NY), 1)
    m = (y == 2 * (k % CY) + k // CY).astype(jnp.float32).astype(jnp.bfloat16)
    for p in range(CZ):
        copies[p].wait()
        r = split_dot(x[p], m) * KAPPA
        for out_ref in (even_ref, odd_ref):
            for s in range(8):
                for j in range(2):
                    out_ref[p, j, pl.ds(s, 8, stride=8), :] = r[8 * s : 8 * s + 8, j * CY : (j + 1) * CY]


def word_kernel(own_ref, out_ref):
    out_ref[...] = own_ref[0, 0, pl.ds(0, 8)]


def gate_kernel(own_ref, word_ref, out_ref):
    del own_ref, word_ref, out_ref


def three(left, mid, right, n):
    def get(p, *rest):
        ref = (left, mid, right)[p // n]
        return ref[(p % n,) + rest]

    return get


def sides(place, n):
    at = jnp.where(place % 2 == 1, 2 * n, 0)
    return at, 2 * n - at


def fine_rounds(own, one, two, put, v, v1, place, blocks):
    for at, ref in zip(sides(place, CZ), (one, two)):
        for p in range(CZ):
            v[at + p] = ref[p]
    get = lambda q, j: own[q - CZ, j] if CZ <= q < 2 * CZ else v[q, j]
    first = place * CZ - WIDE
    n = CZ + 2 * WIDE
    for step in range(WIDE // 2):
        lo = 2 * step + 1
        for p in range(lo, n - lo):
            a, b = fine_euler(get, p, inside(first, p, blocks * CZ, FINE_C))
            v1[p, 0] = a
            v1[p, 1] = b
        for p in range(lo + 1, n - lo - 1):
            a, b = fine_euler(lambda q, j: v1[q, j], p, inside(first, p, blocks * CZ, FINE_C))
            a = 0.5 * (get(p, 0) + a)
            b = 0.5 * (get(p, 1) + b)
            if lo + 1 == WIDE:
                put(p - WIDE, a, b)
            else:
                v[p, 0] = a
                v[p, 1] = b
        get = lambda q, j: v[q, j]


def fine_kernel(blocks, odd, place_ref, own, one, two, out_ref, v, v1):
    def put(p, a, b):
        out_ref[p, 0] = a
        out_ref[p, 1] = b

    @pl.when(place_ref[1] % 2 == odd)
    def _():
        fine_rounds(own, one, two, put, v, v1, place_ref[0], blocks)


def last_fine_kernel(blocks, part, place_ref, own, one, two, co_ref, *refs):
    slab = place_ref[1]
    mine = (slab % 2 == 0, slab == 1, (slab % 2 == 1) & (slab > 1))[part]
    if part:
        out_ref, jump_ref, v, v1 = refs[-4:]
    else:
        out_ref, jump_ref, send_ref, v, v1 = refs

    def put(p, a, b):
        out_ref[p, 0] = a
        out_ref[p, 1] = b

    @pl.when(mine)
    def _():
        fine_rounds(own, one, two, put, v, v1, place_ref[0], blocks)
        for q in range(CC):
            old = co_ref[q]
            jump = restricted(lambda p, j: out_ref[p, j], 2 * q) - old
            jump_ref[q] = jump
            if part == 0:
                send_ref[q] = jnp.where(slab == 0, old + jump, jump)


def coarse_kernel(blocks, place_ref, own0, one0, two0, own1, one1, two1, co_ref, cv, cv1):
    at, then = sides(place_ref[0], CC)

    def fill(ref, base):
        for q in range(CC):
            cv[base + q] = restricted(lambda p, j: ref[p, j], 2 * q)

    for odd, own, one, two in ((0, own0, one0, two0), (1, own1, one1, two1)):

        @pl.when(place_ref[1] % 2 == odd)
        def _():
            fill(own, CC)
            fill(one, at)
            fill(two, then)

    first = (place_ref[0] - 1) * CC
    coarse_propagate(lambda q: cv[q], cv, cv1, 0, 3 * CC, first, blocks * CC)
    for q in range(CC):
        co_ref[q] = cv[CC + q]


def first_sweep_kernel(
    blocks, place_ref, left, mid, right, jump_ref, old_ref, out_ref, send_ref, wide_ref, cv, cv1
):
    at, then = sides(place_ref[0], CC)

    @pl.when(place_ref[1] == 2)
    def _():
        for ref, base in ((jump_ref, CC), (left, at), (right, then)):
            for q in range(CC):
                wide_ref[base + q] = ref[q]

    @pl.when(place_ref[1] > 3)
    def _():
        for n, ref in enumerate((left, mid, right)):
            for q in range(CC):
                wide_ref[n * CC + q] = ref[q]

    @pl.when(place_ref[1] == 1)
    def _():
        first = (place_ref[0] - 1) * CC
        coarse_propagate(three(left, mid, right, CC), cv, cv1, 0, 3 * CC, first, blocks * CC)
        for q in range(CC):
            new = cv[CC + q]
            out_ref[q] = new
            send_ref[q] = new + jump_ref[q]

    @pl.when(place_ref[1] != 1)
    def _():
        out_ref[...] = old_ref[...]
        send_ref[...] = jump_ref[...]


def sweep_kernel(
    blocks, slab, place_ref, a0, a1, a2, a3, a4, wide_ref, jump_ref, old_ref, oldx_ref, *refs
):
    out_ref, outx_ref, send_ref, cv, cv1 = refs[-5:]

    @pl.when(place_ref[1] == slab)
    def _():
        refs = (a0, a1, a2, a3, a4)
        first = (place_ref[0] - 2) * CC
        get = lambda p: refs[p // CC][p % CC]
        coarse_propagate(get, cv, cv1, 0, 5 * CC, first, blocks * CC)
        for q in range(CC):
            outx_ref[q] = cv[2 * CC + q]
        for q in range(CC, 4 * CC):
            cv[q] = cv[q] + wide_ref[q - CC]
        coarse_propagate(lambda q: cv[q], cv, cv1, CC, 4 * CC, first, blocks * CC)
        for q in range(CC):
            new = cv[2 * CC + q]
            out_ref[q] = new
            send_ref[q] = new + jump_ref[q]

    @pl.when(place_ref[1] != slab)
    def _():
        out_ref[...] = old_ref[...]
        outx_ref[...] = oldx_ref[...]
        send_ref[...] = jump_ref[...]


def interleave():
    k = lax.broadcasted_iota(jnp.int32, (NY, NY), 0)
    y = lax.broadcasted_iota(jnp.int32, (NY, NY), 1)
    return (y == 2 * (k % CY) + k // CY).astype(jnp.float32).astype(jnp.bfloat16)


def spread(a):
    return jnp.concatenate([a[8 * (i // 2) : 8 * (i // 2) + 8] for i in range(8)], axis=0)


def rest_kernel(fe_ref, co_ref, out_ref):
    m = interleave()
    for p in range(CZ):
        old = spread(co_ref[p // 2])
        r = jnp.concatenate([fe_ref[p, j] - old for j in range(2)], axis=1)
        r = split_dot(r, m) * (1.0 / KAPPA)
        for h in range(2):
            for i in range(8):
                out_ref[h, p, pl.ds(i, 8, stride=8), :] = r[8 * i : 8 * i + 8, h * CY : (h + 1) * CY]


def final_kernel(place_ref, rest_ref, picked_ref, even_ref, out_ref, x, sems):
    slab = place_ref[1]
    use_even = (slab % 2 == 0) & (slab > 0)
    k = lax.broadcasted_iota(jnp.int32, (CY, NY), 0)
    y = lax.broadcasted_iota(jnp.int32, (CY, NY), 1)
    m = (k == y // 2).astype(jnp.float32).astype(jnp.bfloat16)
    copies = []
    for q in range(CC):
        new = jnp.where(use_even, even_ref[q], picked_ref[q])
        r = split_dot(new, m) * (1.0 / KAPPA)
        for p in (2 * q, 2 * q + 1):
            for h in range(2):
                for i in range(8):
                    at = (h, p, pl.ds(i, 8, stride=8), slice(None))
                    c = 8 * (i // 2)
                    x[at] = rest_ref[at] + r[c : c + 8, h * CY : (h + 1) * CY]
                dst = out_ref.at[0, p, :, pl.ds(h * CY, CY)]
                copies.append(pltpu.make_async_copy(x.at[h, p], dst, sems.at[p, h]))
                copies[-1].start()
    for copy in copies:
        copy.wait()


VM = pl.BlockSpec(memory_space=pltpu.VMEM)
SM = pl.BlockSpec(memory_space=pltpu.SMEM)
HB = pl.BlockSpec(memory_space=pltpu.HBM)
PARAMS = pltpu.CompilerParams(vmem_limit_bytes=VMEM_LIMIT)
fine_shape = jax.ShapeDtypeStruct((CZ, 2, NX, CY), jnp.float32)
half_shape = jax.ShapeDtypeStruct((2, CZ, NX, CY), jnp.float32)
coarse_shape = jax.ShapeDtypeStruct((CC, CX, CY), jnp.float32)
WHOLE = [pltpu.VMEM((CZ, NX, NY), jnp.float32), pltpu.SemaphoreType.DMA((CZ,))]
HALVES = [pltpu.VMEM((2, CZ, NX, CY), jnp.float32), pltpu.SemaphoreType.DMA((CZ, 2))]
FINE_WORK = [pltpu.VMEM((CZ + 2 * WIDE, 2, NX, CY), jnp.float32)] * 2


def coarse_work(n):
    return [pltpu.VMEM((n * CC, CX, CY), jnp.float32)] * 2


def call(kernel, out_shape, in_specs, args, scratch=(), out_specs=None, **kw):
    if out_specs is None:
        out_specs = (VM,) * len(out_shape) if isinstance(out_shape, tuple) else VM
    return pl.pallas_call(
        kernel,
        out_shape=out_shape,
        in_specs=in_specs,
        out_specs=out_specs,
        scratch_shapes=list(scratch),
        compiler_params=PARAMS,
        **kw,
    )(*args)


def both(array, slabs):
    count = lax.axis_size("gz")
    out = []
    for edge in (1, 0):
        pairs = [(k * count + i, k * count + i + 1) for k in slabs for i in range(edge, count - 1, 2)]
        out.append(lax.ppermute(array, ("tm", "gz"), pairs + [(j, i) for i, j in pairs]))
    return out[0], out[1]


def handed(array, slabs, by=0, swap=()):
    count = lax.axis_size("gz")
    pairs = [(a * count + i, b * count + i + by) for a, b in slabs for i in range(count) if 0 <= i + by < count]
    for k in swap:
        for i in range(int(by == 1), count - 1, 2):
            pairs += [(k * count + i, k * count + i + 1), (k * count + i + 1, k * count + i)]
    return lax.ppermute(array, ("tm", "gz"), pairs)


def per_device(start_states):
    blocks = lax.axis_size("gz")
    slabs = lax.axis_size("tm")
    place = jnp.stack([lax.axis_index("gz"), lax.axis_index("tm")]).astype(jnp.int32)
    evens, odds = range(0, slabs, 2), range(1, slabs, 2)
    start_states = pltpu.with_memory_space_constraint(start_states, pltpu.HBM)
    own, own1 = call(prep_kernel, (fine_shape,) * 2, [HB], (start_states,), WHOLE)
    near = both(own, evens)
    word_shape = jax.ShapeDtypeStruct((8, CY), jnp.float32)
    word = handed(call(word_kernel, word_shape, [VM], (own,)), [(k, k + 1) for k in evens])
    own1 = call(gate_kernel, fine_shape, [VM] * 2, (own1, word), input_output_aliases={0: 0})
    near1 = both(own1, odds)
    fine = [SM] + [VM] * 3
    mid = call(functools.partial(fine_kernel, blocks, 0), fine_shape, fine, (place, own, *near), FINE_WORK)
    next0 = both(mid, evens)
    mid1 = call(functools.partial(fine_kernel, blocks, 1), fine_shape, fine, (place, own1, *near1), FINE_WORK)
    next1 = both(mid1, odds)
    old = call(
        functools.partial(coarse_kernel, blocks),
        coarse_shape,
        [SM] + [VM] * 6,
        (place, own, *near, own1, *near1),
        coarse_work(3),
    )
    fine_end, jump, send = call(
        functools.partial(last_fine_kernel, blocks, 0),
        (fine_shape, coarse_shape, coarse_shape),
        [SM] + [VM] * 4,
        (place, mid, *next0, old),
        FINE_WORK,
    )
    fine_end, jump = call(
        functools.partial(last_fine_kernel, blocks, 1),
        (fine_shape, coarse_shape),
        [SM] + [VM] * 6,
        (place, mid1, *next1, old, fine_end, jump),
        FINE_WORK,
        input_output_aliases={5: 0, 6: 1},
    )
    firsts = range(0, slabs - 1, 2)
    pairs = [(k, k + 1) for k in firsts if k != 2]
    side = [handed(send, pairs, by, (2,) if by else ()) for by in (1, 0, -1)]
    wide_shape = jax.ShapeDtypeStruct((3 * CC, CX, CY), jnp.float32)
    picked, send, wide = call(
        functools.partial(first_sweep_kernel, blocks),
        (coarse_shape, coarse_shape, wide_shape),
        [SM] + [VM] * 5,
        (place, *side, jump, old),
        coarse_work(3),
    )
    fine_end, jump = call(
        functools.partial(last_fine_kernel, blocks, 2),
        (fine_shape, coarse_shape),
        [SM] + [VM] * 7,
        (place, mid1, *next1, old, fine_end, jump, send),
        FINE_WORK,
        input_output_aliases={5: 0, 6: 1},
    )
    rest = call(rest_kernel, half_shape, [VM] * 2, (fine_end, old))
    even = jump
    for k in firsts[1:]:
        early = (rest,) if k == firsts[-1] else ()
        got = [handed(send, [(k - 1, k + 1)], by) for by in (2, 1, 0, -1, -2)]
        near = wide
        if k == 2:
            near, jump, *got = lax.optimization_barrier((wide, jump, *got))
            near = handed(near, [(2, 3)])
        picked, even, send = call(
            functools.partial(sweep_kernel, blocks, k + 1),
            (coarse_shape,) * 3,
            [SM] + [VM] * 9 + [HB] * len(early),
            (place, *got, near, jump, picked, even, *early),
            coarse_work(5),
        )
    even = handed(even, [(k + 1, k) for k in firsts[1:]])
    return call(
        final_kernel,
        jax.ShapeDtypeStruct((1, CZ, NX, NY), jnp.float32),
        [SM] + [VM] * 3,
        (place, rest, picked, even),
        HALVES,
        HB,
    )


def solution(mesh):
    placed = (P("tm", "gz", None, None),)
    return jax.shard_map(
        per_device, mesh=mesh, in_specs=placed, out_specs=P("tm", "gz", None, None), check_vma=False
    )
```

```python
import functools
import math

import jax
import jax.numpy as jnp
from jax import lax
from jax.experimental import pallas as pl
from jax.experimental.pallas import tpu as pltpu
from jax.sharding import PartitionSpec as P

COARSE_STEPS = 2
FINE_STEPS = 8

fine_dt = 0.025
coarse_dt = 0.1
fine_coef = 4.8
coarse_coef = 1.2

KAPPA = math.sqrt(fine_dt)
FINE_A = 1.0 + fine_dt * (1.0 - 6.0 * fine_coef)
FINE_C = fine_dt * fine_coef
COARSE_A = 1.0 + coarse_dt * (1.0 - 6.0 * coarse_coef)
COARSE_B = coarse_dt / fine_dt
COARSE_C = coarse_dt * coarse_coef

CZ, NX, NY = 8, 64, 256
ROUNDS = 2
WIDE = 2 * FINE_STEPS // ROUNDS
CC, CX, CY = CZ // 2, NX // 2, NY // 2
REACH = 2 * COARSE_STEPS
VMEM_LIMIT = 40 * 1024 * 1024


def x_sum(a):
    n = a.shape[0]
    after = jnp.concatenate([a[8:], pltpu.roll(a[:8], 7, 0)], axis=0)
    before = jnp.concatenate([pltpu.roll(a[n - 8 :], 1, 0), a[: n - 8]], axis=0)
    return after + before


def split_dot(a, m):
    hi = a.astype(jnp.bfloat16)
    rest = a - hi.astype(jnp.float32)
    mid = rest.astype(jnp.bfloat16)
    low = (rest - mid.astype(jnp.float32)).astype(jnp.bfloat16)
    dot = functools.partial(jnp.dot, preferred_element_type=jnp.float32)
    return dot(hi, m) + (dot(mid, m) + dot(low, m))


def fine_euler(get, p, c):
    out = []
    for j, by in ((0, 1), (1, CY - 1)):
        a = get(p, j)
        b = get(p, 1 - j)
        total = (get(p - 1, j) + get(p + 1, j)) + (x_sum(a) + (b + pltpu.roll(b, by, 1)))
        out.append(c * total + a * (FINE_A - a * a))
    return out


def coarse_euler(get, p, c):
    a = get(p)
    total = (get(p - 1) + get(p + 1)) + (x_sum(a) + (pltpu.roll(a, 1, 1) + pltpu.roll(a, CY - 1, 1)))
    return c * total + a * (COARSE_A - COARSE_B * (a * a))


def inside(first, p, count, coef):
    g = first + p
    return jnp.where((g >= 0) & (g < count), coef, 0.0).astype(jnp.float32)


def coarse_propagate(get, v, v1, lo, hi, first, count):
    for step in range(COARSE_STEPS):
        lo, hi = lo + 1, hi - 1
        for p in range(lo, hi):
            v1[p] = coarse_euler(get, p, inside(first, p, count, COARSE_C))
        lo, hi = lo + 1, hi - 1
        for p in range(lo, hi):
            new = coarse_euler(lambda q: v1[q], p, inside(first, p, count, COARSE_C))
            v[p] = 0.5 * (get(p) + new)
        get = lambda q: v[q]


def restricted(get, p):
    s = (get(p, 0) + get(p + 1, 0)) + (get(p, 1) + get(p + 1, 1))
    rows = [s[16 * i : 16 * i + 8] + s[16 * i + 8 : 16 * i + 16] for i in range(4)]
    return 0.125 * jnp.concatenate(rows, axis=0)


def prep_kernel(x_ref, out_ref, x, sems):
    copies = [pltpu.make_async_copy(x_ref.at[0, p], x.at[p], sems.at[p]) for p in range(CZ)]
    for copy in copies:
        copy.start()
    y = lax.broadcasted_iota(jnp.int32, (NY, NY), 0)
    k = lax.broadcasted_iota(jnp.int32, (NY, NY), 1)
    m = (y == 2 * (k % CY) + k // CY).astype(jnp.float32).astype(jnp.bfloat16)
    for p in range(CZ):
        copies[p].wait()
        r = split_dot(x[p], m) * KAPPA
        for s in range(8):
            for j in range(2):
                out_ref[p, j, pl.ds(s, 8, stride=8), :] = r[8 * s : 8 * s + 8, j * CY : (j + 1) * CY]


def word_kernel(own_ref, out_ref):
    out_ref[...] = own_ref[0, 0, pl.ds(0, 8)]


def three(left, mid, right, n):
    def get(p, *rest):
        ref = (left, mid, right)[p // n]
        return ref[(p % n,) + rest]

    return get


def sides(place, n):
    at = jnp.where(place % 2 == 1, 2 * n, 0)
    return at, 2 * n - at


def fine_rounds(own, one, two, put, v, v1, place, blocks):
    for at, ref in zip(sides(place, CZ), (one, two)):
        for p in range(CZ):
            v[at + p] = ref[p]
    get = lambda q, j: own[q - CZ, j] if CZ <= q < 2 * CZ else v[q, j]
    first = place * CZ - WIDE
    n = CZ + 2 * WIDE
    for step in range(WIDE // 2):
        lo = 2 * step + 1
        for p in range(lo, n - lo):
            a, b = fine_euler(get, p, inside(first, p, blocks * CZ, FINE_C))
            v1[p, 0] = a
            v1[p, 1] = b
        for p in range(lo + 1, n - lo - 1):
            a, b = fine_euler(lambda q, j: v1[q, j], p, inside(first, p, blocks * CZ, FINE_C))
            a = 0.5 * (get(p, 0) + a)
            b = 0.5 * (get(p, 1) + b)
            if lo + 1 == WIDE:
                put(p - WIDE, a, b)
            else:
                v[p, 0] = a
                v[p, 1] = b
        get = lambda q, j: v[q, j]


def fine_kernel(blocks, odd, place_ref, own, one, two, *refs):
    out_ref, v, v1 = refs[-3:]

    def put(p, a, b):
        out_ref[p, 0] = a
        out_ref[p, 1] = b

    @pl.when(place_ref[1] % 2 == odd)
    def _():
        fine_rounds(own, one, two, put, v, v1, place_ref[0], blocks)


def last_fine_kernel(blocks, part, place_ref, own, one, two, co_ref, *refs):
    slab = place_ref[1]
    mine = (slab % 2 == 0, slab == 1, slab == 3, (slab % 2 == 1) & (slab > 3))[part]
    if part:
        out_ref, jump_ref, v, v1 = refs[-4:]
    else:
        out_ref, jump_ref, send_ref, v, v1 = refs

    def put(p, a, b):
        out_ref[p, 0] = a
        out_ref[p, 1] = b

    @pl.when(mine)
    def _():
        fine_rounds(own, one, two, put, v, v1, place_ref[0], blocks)
        for q in range(CC):
            old = co_ref[q]
            jump = restricted(lambda p, j: out_ref[p, j], 2 * q) - old
            jump_ref[q] = jump
            if part == 0:
                send_ref[q] = jnp.where(slab == 0, old + jump, jump)


def coarse_kernel(blocks, place_ref, own, one0, two0, one1, two1, co_ref, cv, cv1):
    at, then = sides(place_ref[0], CC)

    def fill(ref, base):
        for q in range(CC):
            cv[base + q] = restricted(lambda p, j: ref[p, j], 2 * q)

    fill(own, CC)
    for odd, one, two in ((0, one0, two0), (1, one1, two1)):

        @pl.when(place_ref[1] % 2 == odd)
        def _():
            fill(one, at)
            fill(two, then)

    first = (place_ref[0] - 1) * CC
    coarse_propagate(lambda q: cv[q], cv, cv1, 0, 3 * CC, first, blocks * CC)
    for q in range(CC):
        co_ref[q] = cv[CC + q]


def first_sweep_kernel(
    blocks, place_ref, mid, left, right, jump_ref, old_ref, out_ref, send_ref, wide_ref, cv, cv1
):
    at, then = sides(place_ref[0], CC)

    @pl.when(place_ref[1] == 2)
    def _():
        for ref, base in ((jump_ref, CC), (left, at), (right, then)):
            for q in range(CC):
                wide_ref[base + q] = ref[q]

    @pl.when(place_ref[1] > 3)
    def _():
        for n, ref in enumerate((left, mid, right)):
            for q in range(CC):
                wide_ref[n * CC + q] = ref[q]

    @pl.when(place_ref[1] == 1)
    def _():
        first = (place_ref[0] - 1) * CC
        coarse_propagate(three(left, mid, right, CC), cv, cv1, 0, 3 * CC, first, blocks * CC)
        for q in range(CC):
            new = cv[CC + q]
            out_ref[q] = new
            send_ref[q] = new + jump_ref[q]

    @pl.when(place_ref[1] != 1)
    def _():
        out_ref[...] = old_ref[...]
        send_ref[...] = jump_ref[...]


def sweep_kernel(
    blocks, slab, place_ref, a0, a4, a1, a3, a2, wide_ref, jump_ref, old_ref, oldx_ref, *refs
):
    out_ref, outx_ref, send_ref, cv, cv1 = refs[-5:]

    @pl.when(place_ref[1] == slab)
    def _():
        refs = (a0, a1, a2, a3, a4)
        first = (place_ref[0] - 2) * CC
        get = lambda p: refs[p // CC][p % CC]
        coarse_propagate(get, cv, cv1, 0, 5 * CC, first, blocks * CC)
        for q in range(CC):
            outx_ref[q] = cv[2 * CC + q]
        for q in range(CC, 4 * CC):
            cv[q] = cv[q] + wide_ref[q - CC]
        coarse_propagate(lambda q: cv[q], cv, cv1, CC, 4 * CC, first, blocks * CC)
        for q in range(CC):
            new = cv[2 * CC + q]
            out_ref[q] = new
            send_ref[q] = new + jump_ref[q]

    @pl.when(place_ref[1] != slab)
    def _():
        out_ref[...] = old_ref[...]
        outx_ref[...] = oldx_ref[...]
        send_ref[...] = jump_ref[...]


def even_sweep_kernel(blocks, slab, place_ref, a0, a4, a1, a3, a2, oldx_ref, *refs):
    outx_ref, next_ref, cv, cv1 = refs[-4:]

    @pl.when(place_ref[1] == slab)
    def _():
        refs = (a0, a1, a2, a3, a4)
        first = (place_ref[0] - 2) * CC
        coarse_propagate(lambda p: refs[p // CC][p % CC], cv, cv1, 0, 5 * CC, first, blocks * CC)
        for q in range(CC):
            outx_ref[q] = cv[2 * CC + q]
        for q in range(3 * CC):
            next_ref[q] = cv[CC + q]

    @pl.when(place_ref[1] != slab)
    def _():
        outx_ref[...] = oldx_ref[...]


def odd_sweep_kernel(blocks, slab, place_ref, next_ref, wide_ref, jump_ref, old_ref, out_ref, send_ref, cv, cv1):
    @pl.when(place_ref[1] == slab)
    def _():
        for q in range(3 * CC):
            cv[q] = next_ref[q] + wide_ref[q]
        first = (place_ref[0] - 1) * CC
        coarse_propagate(lambda q: cv[q], cv, cv1, 0, 3 * CC, first, blocks * CC)
        for q in range(CC):
            new = cv[CC + q]
            out_ref[q] = new
            send_ref[q] = new + jump_ref[q]

    @pl.when(place_ref[1] != slab)
    def _():
        out_ref[...] = old_ref[...]
        send_ref[...] = jump_ref[...]


def interleave():
    k = lax.broadcasted_iota(jnp.int32, (NY, NY), 0)
    y = lax.broadcasted_iota(jnp.int32, (NY, NY), 1)
    return (y == 2 * (k % CY) + k // CY).astype(jnp.float32).astype(jnp.bfloat16)


def spread(a):
    return jnp.concatenate([a[8 * (i // 2) : 8 * (i // 2) + 8] for i in range(8)], axis=0)


def rest_kernel(fe_ref, co_ref, out_ref):
    m = interleave()
    for p in range(CZ):
        old = spread(co_ref[p // 2])
        r = jnp.concatenate([fe_ref[p, j] - old for j in range(2)], axis=1)
        r = split_dot(r, m) * (1.0 / KAPPA)
        for h in range(2):
            for i in range(8):
                out_ref[h, p, pl.ds(i, 8, stride=8), :] = r[8 * i : 8 * i + 8, h * CY : (h + 1) * CY]


def final_kernel(place_ref, rest_ref, picked_ref, even_ref, out_ref, x, sems):
    slab = place_ref[1]
    use_even = (slab % 2 == 0) & (slab > 0)
    k = lax.broadcasted_iota(jnp.int32, (CY, NY), 0)
    y = lax.broadcasted_iota(jnp.int32, (CY, NY), 1)
    m = (k == y // 2).astype(jnp.float32).astype(jnp.bfloat16)
    copies = []
    for q in range(CC):
        new = jnp.where(use_even, even_ref[q], picked_ref[q])
        r = split_dot(new, m) * (1.0 / KAPPA)
        for p in (2 * q, 2 * q + 1):
            for h in range(2):
                for i in range(8):
                    at = (h, p, pl.ds(i, 8, stride=8), slice(None))
                    c = 8 * (i // 2)
                    x[at] = rest_ref[at] + r[c : c + 8, h * CY : (h + 1) * CY]
                dst = out_ref.at[0, p, :, pl.ds(h * CY, CY)]
                copies.append(pltpu.make_async_copy(x.at[h, p], dst, sems.at[p, h]))
                copies[-1].start()
    for copy in copies:
        copy.wait()


VM = pl.BlockSpec(memory_space=pltpu.VMEM)
SM = pl.BlockSpec(memory_space=pltpu.SMEM)
HB = pl.BlockSpec(memory_space=pltpu.HBM)
PARAMS = pltpu.CompilerParams(vmem_limit_bytes=VMEM_LIMIT)
fine_shape = jax.ShapeDtypeStruct((CZ, 2, NX, CY), jnp.float32)
half_shape = jax.ShapeDtypeStruct((2, CZ, NX, CY), jnp.float32)
coarse_shape = jax.ShapeDtypeStruct((CC, CX, CY), jnp.float32)
WHOLE = [pltpu.VMEM((CZ, NX, NY), jnp.float32), pltpu.SemaphoreType.DMA((CZ,))]
HALVES = [pltpu.VMEM((2, CZ, NX, CY), jnp.float32), pltpu.SemaphoreType.DMA((CZ, 2))]
FINE_WORK = [pltpu.VMEM((CZ + 2 * WIDE, 2, NX, CY), jnp.float32)] * 2


def coarse_work(n):
    return [pltpu.VMEM((n * CC, CX, CY), jnp.float32)] * 2


def call(kernel, out_shape, in_specs, args, scratch=(), out_specs=None, **kw):
    if out_specs is None:
        out_specs = (VM,) * len(out_shape) if isinstance(out_shape, tuple) else VM
    return pl.pallas_call(
        kernel,
        out_shape=out_shape,
        in_specs=in_specs,
        out_specs=out_specs,
        scratch_shapes=list(scratch),
        compiler_params=PARAMS,
        **kw,
    )(*args)


def both(array, slabs):
    count = lax.axis_size("gz")
    out = []
    for edge in (1, 0):
        pairs = [(k * count + i, k * count + i + 1) for k in slabs for i in range(edge, count - 1, 2)]
        out.append(lax.ppermute(array, ("tm", "gz"), pairs + [(j, i) for i, j in pairs]))
    return out[0], out[1]


def handed(array, slabs, by=0, swap=()):
    count = lax.axis_size("gz")
    pairs = [(a * count + i, b * count + i + by) for a, b in slabs for i in range(count) if 0 <= i + by < count]
    for k in swap:
        for i in range(int(by == 1), count - 1, 2):
            pairs += [(k * count + i, k * count + i + 1), (k * count + i + 1, k * count + i)]
    return lax.ppermute(array, ("tm", "gz"), pairs)


def per_device(start_states):
    blocks = lax.axis_size("gz")
    slabs = lax.axis_size("tm")
    place = jnp.stack([lax.axis_index("gz"), lax.axis_index("tm")]).astype(jnp.int32)
    evens, odds = range(0, slabs, 2), range(1, slabs, 2)
    start_states = pltpu.with_memory_space_constraint(start_states, pltpu.HBM)
    own = call(prep_kernel, fine_shape, [HB], (start_states,), WHOLE)
    near = both(own, evens)
    word_shape = jax.ShapeDtypeStruct((8, CY), jnp.float32)
    word = handed(call(word_kernel, word_shape, [VM], (own,)), [(k, k + 1) for k in evens])
    own1, word = lax.optimization_barrier((own, word))
    near1 = both(own1, odds)
    fine = [SM] + [VM] * 3
    mid = call(functools.partial(fine_kernel, blocks, 0), fine_shape, fine, (place, own, *near), FINE_WORK)
    next0 = both(mid, evens)
    mid1 = call(
        functools.partial(fine_kernel, blocks, 1), fine_shape, fine + [HB], (place, own1, *near1, word), FINE_WORK
    )
    next1 = both(mid1, odds)
    old = call(
        functools.partial(coarse_kernel, blocks),
        coarse_shape,
        [SM] + [VM] * 5,
        (place, own, *near, *near1),
        coarse_work(3),
    )
    fine_end, jump, send = call(
        functools.partial(last_fine_kernel, blocks, 0),
        (fine_shape, coarse_shape, coarse_shape),
        [SM] + [VM] * 4,
        (place, mid, *next0, old),
        FINE_WORK,
    )
    fine_end, jump = call(
        functools.partial(last_fine_kernel, blocks, 1),
        (fine_shape, coarse_shape),
        [SM] + [VM] * 6,
        (place, mid1, *next1, old, fine_end, jump),
        FINE_WORK,
        input_output_aliases={5: 0, 6: 1},
    )
    firsts = range(0, slabs - 1, 2)
    pairs = [(k, k + 1) for k in firsts if k != 2]
    side = [handed(send, pairs, by, (2,) if by else ()) for by in (0, 1, -1)]
    wide_shape = jax.ShapeDtypeStruct((3 * CC, CX, CY), jnp.float32)
    picked, send, wide = call(
        functools.partial(first_sweep_kernel, blocks),
        (coarse_shape, coarse_shape, wide_shape),
        [SM] + [VM] * 5,
        (place, *side, jump, old),
        coarse_work(3),
    )

    def end_fine(part, *after):
        return call(
            functools.partial(last_fine_kernel, blocks, part),
            (fine_shape, coarse_shape),
            [SM] + [VM] * 6 + [HB] * len(after),
            (place, mid1, *next1, old, fine_end, jump, *after),
            FINE_WORK,
            input_output_aliases={5: 0, 6: 1},
        )

    fine_end, jump = end_fine(2, send)
    even = old
    for k in firsts[1:]:
        if k == 4:
            fine_end, jump = end_fine(3, send)
            rest = call(rest_kernel, half_shape, [VM] * 2, (fine_end, old))
        early = (rest,) if k == firsts[-1] else ()
        got = [handed(send, [(k - 1, k + 1)], by) for by in (2, -2, 1, -1, 0)]
        near = wide
        if k == 2:
            near, jump, *got = lax.optimization_barrier((wide, jump, *got))
            near = handed(near, [(2, 3)])
        if k == 2:
            even, state = call(
                functools.partial(even_sweep_kernel, blocks, k + 1),
                (coarse_shape, wide_shape),
                [SM] + [VM] * 6 + [HB] * len(early),
                (place, *got, even, *early),
                coarse_work(5),
            )
            picked, send = call(
                functools.partial(odd_sweep_kernel, blocks, k + 1),
                (coarse_shape,) * 2,
                [SM] + [VM] * 4,
                (place, state, near, jump, picked),
                coarse_work(3),
            )
        else:
            picked, even, send = call(
                functools.partial(sweep_kernel, blocks, k + 1),
                (coarse_shape,) * 3,
                [SM] + [VM] * 9 + [HB] * len(early),
                (place, *got, near, jump, picked, even, *early),
                coarse_work(5),
            )
    even = handed(even, [(k + 1, k) for k in firsts[1:]])
    return call(
        final_kernel,
        jax.ShapeDtypeStruct((1, CZ, NX, NY), jnp.float32),
        [SM] + [VM] * 3,
        (place, rest, picked, even),
        HALVES,
        HB,
    )


def solution(mesh):
    placed = (P("tm", "gz", None, None),)
    return jax.shard_map(
        per_device, mesh=mesh, in_specs=placed, out_specs=P("tm", "gz", None, None), check_vma=False
    )
```

```python
import functools
import math

import jax
import jax.numpy as jnp
from jax import lax
from jax.experimental import pallas as pl
from jax.experimental.pallas import tpu as pltpu
from jax.sharding import PartitionSpec as P

COARSE_STEPS = 2
FINE_STEPS = 8

fine_dt = 0.025
coarse_dt = 0.1
fine_coef = 4.8
coarse_coef = 1.2

KAPPA = math.sqrt(fine_dt)
FINE_A = 1.0 + fine_dt * (1.0 - 6.0 * fine_coef)
FINE_C = fine_dt * fine_coef
COARSE_A = 1.0 + coarse_dt * (1.0 - 6.0 * coarse_coef)
COARSE_B = coarse_dt / fine_dt
COARSE_C = coarse_dt * coarse_coef

CZ, NX, NY = 8, 64, 256
ROUNDS = 2
WIDE = 2 * FINE_STEPS // ROUNDS
CC, CX, CY = CZ // 2, NX // 2, NY // 2
REACH = 2 * COARSE_STEPS
VMEM_LIMIT = 40 * 1024 * 1024


def x_sum(a):
    n = a.shape[0]
    after = jnp.concatenate([a[8:], pltpu.roll(a[:8], 7, 0)], axis=0)
    before = jnp.concatenate([pltpu.roll(a[n - 8 :], 1, 0), a[: n - 8]], axis=0)
    return after + before


def split_dot(a, m):
    hi = a.astype(jnp.bfloat16)
    rest = a - hi.astype(jnp.float32)
    mid = rest.astype(jnp.bfloat16)
    low = (rest - mid.astype(jnp.float32)).astype(jnp.bfloat16)
    dot = functools.partial(jnp.dot, preferred_element_type=jnp.float32)
    return dot(hi, m) + (dot(mid, m) + dot(low, m))


def fine_euler(get, p, c):
    out = []
    for j, by in ((0, 1), (1, CY - 1)):
        a = get(p, j)
        b = get(p, 1 - j)
        total = (get(p - 1, j) + get(p + 1, j)) + (x_sum(a) + (b + pltpu.roll(b, by, 1)))
        out.append(c * total + a * (FINE_A - a * a))
    return out


def coarse_euler(get, p, c):
    a = get(p)
    total = (get(p - 1) + get(p + 1)) + (x_sum(a) + (pltpu.roll(a, 1, 1) + pltpu.roll(a, CY - 1, 1)))
    return c * total + a * (COARSE_A - COARSE_B * (a * a))


def inside(first, p, count, coef):
    g = first + p
    return jnp.where((g >= 0) & (g < count), coef, 0.0).astype(jnp.float32)


def coarse_propagate(get, v, v1, lo, hi, first, count):
    for step in range(COARSE_STEPS):
        lo, hi = lo + 1, hi - 1
        for p in range(lo, hi):
            v1[p] = coarse_euler(get, p, inside(first, p, count, COARSE_C))
        lo, hi = lo + 1, hi - 1
        for p in range(lo, hi):
            new = coarse_euler(lambda q: v1[q], p, inside(first, p, count, COARSE_C))
            v[p] = 0.5 * (get(p) + new)
        get = lambda q: v[q]


def restricted(get, p):
    s = (get(p, 0) + get(p + 1, 0)) + (get(p, 1) + get(p + 1, 1))
    rows = [s[16 * i : 16 * i + 8] + s[16 * i + 8 : 16 * i + 16] for i in range(4)]
    return 0.125 * jnp.concatenate(rows, axis=0)


def prep_kernel(x_ref, out_ref, x, sems):
    copies = [pltpu.make_async_copy(x_ref.at[0, p], x.at[p], sems.at[p]) for p in range(CZ)]
    for copy in copies:
        copy.start()
    y = lax.broadcasted_iota(jnp.int32, (NY, NY), 0)
    k = lax.broadcasted_iota(jnp.int32, (NY, NY), 1)
    m = (y == 2 * (k % CY) + k // CY).astype(jnp.float32).astype(jnp.bfloat16)
    for p in range(CZ):
        copies[p].wait()
        r = split_dot(x[p], m) * KAPPA
        for s in range(8):
            for j in range(2):
                out_ref[p, j, pl.ds(s, 8, stride=8), :] = r[8 * s : 8 * s + 8, j * CY : (j + 1) * CY]


def word_kernel(own_ref, out_ref):
    out_ref[...] = own_ref[0, 0, pl.ds(0, 8)]


def three(left, mid, right, n):
    def get(p, *rest):
        ref = (left, mid, right)[p // n]
        return ref[(p % n,) + rest]

    return get


def sides(place, n):
    at = jnp.where(place % 2 == 1, 2 * n, 0)
    return at, 2 * n - at


def fine_rounds(own, one, two, put, v, v1, place, blocks):
    for at, ref in zip(sides(place, CZ), (one, two)):
        for p in range(CZ):
            v[at + p] = ref[p]
    get = lambda q, j: own[q - CZ, j] if CZ <= q < 2 * CZ else v[q, j]
    first = place * CZ - WIDE
    n = CZ + 2 * WIDE
    for step in range(WIDE // 2):
        lo = 2 * step + 1
        for p in range(lo, n - lo):
            a, b = fine_euler(get, p, inside(first, p, blocks * CZ, FINE_C))
            v1[p, 0] = a
            v1[p, 1] = b
        for p in range(lo + 1, n - lo - 1):
            a, b = fine_euler(lambda q, j: v1[q, j], p, inside(first, p, blocks * CZ, FINE_C))
            a = 0.5 * (get(p, 0) + a)
            b = 0.5 * (get(p, 1) + b)
            if lo + 1 == WIDE:
                put(p - WIDE, a, b)
            else:
                v[p, 0] = a
                v[p, 1] = b
        get = lambda q, j: v[q, j]


def fine_kernel(blocks, odd, place_ref, own, one, two, *refs):
    out_ref, v, v1 = refs[-3:]

    def put(p, a, b):
        out_ref[p, 0] = a
        out_ref[p, 1] = b

    @pl.when(place_ref[1] % 2 == odd)
    def _():
        fine_rounds(own, one, two, put, v, v1, place_ref[0], blocks)


def last_fine_kernel(blocks, part, place_ref, own, one, two, co_ref, *refs):
    slab = place_ref[1]
    mine = (slab % 2 == 0, slab == 1, slab == 3, (slab % 2 == 1) & (slab > 3))[part]
    if part:
        out_ref, jump_ref, v, v1 = refs[-4:]
    else:
        out_ref, jump_ref, send_ref, v, v1 = refs

    def put(p, a, b):
        out_ref[p, 0] = a
        out_ref[p, 1] = b

    @pl.when(mine)
    def _():
        fine_rounds(own, one, two, put, v, v1, place_ref[0], blocks)
        for q in range(CC):
            old = co_ref[q]
            jump = restricted(lambda p, j: out_ref[p, j], 2 * q) - old
            jump_ref[q] = jump
            if part == 0:
                send_ref[q] = jnp.where(slab == 0, old + jump, jump)


def coarse_kernel(blocks, place_ref, own, one0, two0, one1, two1, co_ref, cv, cv1):
    at, then = sides(place_ref[0], CC)

    def fill(ref, base):
        for q in range(CC):
            cv[base + q] = restricted(lambda p, j: ref[p, j], 2 * q)

    fill(own, CC)
    for odd, one, two in ((0, one0, two0), (1, one1, two1)):

        @pl.when(place_ref[1] % 2 == odd)
        def _():
            fill(one, at)
            fill(two, then)

    first = (place_ref[0] - 1) * CC
    coarse_propagate(lambda q: cv[q], cv, cv1, 0, 3 * CC, first, blocks * CC)
    for q in range(CC):
        co_ref[q] = cv[CC + q]


def first_sweep_kernel(
    blocks, place_ref, mid, left, right, jump_ref, old_ref, out_ref, send_ref, wide_ref, cv, cv1
):
    at, then = sides(place_ref[0], CC)

    @pl.when(place_ref[1] == 2)
    def _():
        for ref, base in ((jump_ref, CC), (left, at), (right, then)):
            for q in range(CC):
                wide_ref[base + q] = ref[q]

    @pl.when(place_ref[1] > 3)
    def _():
        for n, ref in enumerate((left, mid, right)):
            for q in range(CC):
                wide_ref[n * CC + q] = ref[q]

    @pl.when(place_ref[1] == 1)
    def _():
        first = (place_ref[0] - 1) * CC
        coarse_propagate(three(left, mid, right, CC), cv, cv1, 0, 3 * CC, first, blocks * CC)
        for q in range(CC):
            new = cv[CC + q]
            out_ref[q] = new
            send_ref[q] = new + jump_ref[q]

    @pl.when(place_ref[1] != 1)
    def _():
        out_ref[...] = old_ref[...]
        send_ref[...] = jump_ref[...]


def sweep_kernel(
    blocks, slab, place_ref, a0, a4, a1, a3, a2, wide_ref, jump_ref, old_ref, oldx_ref, *refs
):
    out_ref, outx_ref, send_ref, cv, cv1 = refs[-5:]

    @pl.when(place_ref[1] == slab)
    def _():
        refs = (a0, a1, a2, a3, a4)
        first = (place_ref[0] - 2) * CC
        get = lambda p: refs[p // CC][p % CC]
        coarse_propagate(get, cv, cv1, 0, 5 * CC, first, blocks * CC)
        for q in range(CC):
            outx_ref[q] = cv[2 * CC + q]
        for q in range(CC, 4 * CC):
            cv[q] = cv[q] + wide_ref[q - CC]
        coarse_propagate(lambda q: cv[q], cv, cv1, CC, 4 * CC, first, blocks * CC)
        for q in range(CC):
            new = cv[2 * CC + q]
            out_ref[q] = new
            send_ref[q] = new + jump_ref[q]

    @pl.when(place_ref[1] != slab)
    def _():
        out_ref[...] = old_ref[...]
        outx_ref[...] = oldx_ref[...]
        send_ref[...] = jump_ref[...]


def even_sweep_kernel(blocks, slab, place_ref, a0, a4, a1, a3, a2, oldx_ref, *refs):
    outx_ref, next_ref, cv, cv1 = refs[-4:]

    @pl.when(place_ref[1] == slab)
    def _():
        refs = (a0, a1, a2, a3, a4)
        first = (place_ref[0] - 2) * CC
        coarse_propagate(lambda p: refs[p // CC][p % CC], cv, cv1, 0, 5 * CC, first, blocks * CC)
        for q in range(CC):
            outx_ref[q] = cv[2 * CC + q]
        for q in range(3 * CC):
            next_ref[q] = cv[CC + q]

    @pl.when(place_ref[1] != slab)
    def _():
        outx_ref[...] = oldx_ref[...]


def odd_sweep_kernel(blocks, slab, place_ref, next_ref, wide_ref, jump_ref, old_ref, out_ref, send_ref, cv, cv1):
    @pl.when(place_ref[1] == slab)
    def _():
        for q in range(3 * CC):
            cv[q] = next_ref[q] + wide_ref[q]
        first = (place_ref[0] - 1) * CC
        coarse_propagate(lambda q: cv[q], cv, cv1, 0, 3 * CC, first, blocks * CC)
        for q in range(CC):
            new = cv[CC + q]
            out_ref[q] = new
            send_ref[q] = new + jump_ref[q]

    @pl.when(place_ref[1] != slab)
    def _():
        out_ref[...] = old_ref[...]
        send_ref[...] = jump_ref[...]


def interleave():
    k = lax.broadcasted_iota(jnp.int32, (NY, NY), 0)
    y = lax.broadcasted_iota(jnp.int32, (NY, NY), 1)
    return (y == 2 * (k % CY) + k // CY).astype(jnp.float32).astype(jnp.bfloat16)


def spread(a):
    return jnp.concatenate([a[8 * (i // 2) : 8 * (i // 2) + 8] for i in range(8)], axis=0)


def rest_kernel(fe_ref, co_ref, out_ref):
    m = interleave()
    for p in range(CZ):
        old = spread(co_ref[p // 2])
        r = jnp.concatenate([fe_ref[p, j] - old for j in range(2)], axis=1)
        r = split_dot(r, m) * (1.0 / KAPPA)
        for h in range(2):
            for i in range(8):
                out_ref[h, p, pl.ds(i, 8, stride=8), :] = r[8 * i : 8 * i + 8, h * CY : (h + 1) * CY]


def final_kernel(place_ref, rest_ref, picked_ref, even_ref, out_ref, x, sems):
    slab = place_ref[1]
    use_even = (slab % 2 == 0) & (slab > 0)
    k = lax.broadcasted_iota(jnp.int32, (CY, NY), 0)
    y = lax.broadcasted_iota(jnp.int32, (CY, NY), 1)
    m = (k == y // 2).astype(jnp.float32).astype(jnp.bfloat16)
    copies = []
    for q in range(CC):
        new = jnp.where(use_even, even_ref[q], picked_ref[q])
        r = split_dot(new, m) * (1.0 / KAPPA)
        for p in (2 * q, 2 * q + 1):
            for h in range(2):
                for i in range(8):
                    at = (h, p, pl.ds(i, 8, stride=8), slice(None))
                    c = 8 * (i // 2)
                    x[at] = rest_ref[at] + r[c : c + 8, h * CY : (h + 1) * CY]
                dst = out_ref.at[0, p, :, pl.ds(h * CY, CY)]
                copies.append(pltpu.make_async_copy(x.at[h, p], dst, sems.at[p, h]))
                copies[-1].start()
    for copy in copies:
        copy.wait()


VM = pl.BlockSpec(memory_space=pltpu.VMEM)
SM = pl.BlockSpec(memory_space=pltpu.SMEM)
HB = pl.BlockSpec(memory_space=pltpu.HBM)
PARAMS = pltpu.CompilerParams(vmem_limit_bytes=VMEM_LIMIT)
fine_shape = jax.ShapeDtypeStruct((CZ, 2, NX, CY), jnp.float32)
half_shape = jax.ShapeDtypeStruct((2, CZ, NX, CY), jnp.float32)
coarse_shape = jax.ShapeDtypeStruct((CC, CX, CY), jnp.float32)
WHOLE = [pltpu.VMEM((CZ, NX, NY), jnp.float32), pltpu.SemaphoreType.DMA((CZ,))]
HALVES = [pltpu.VMEM((2, CZ, NX, CY), jnp.float32), pltpu.SemaphoreType.DMA((CZ, 2))]
FINE_WORK = [pltpu.VMEM((CZ + 2 * WIDE, 2, NX, CY), jnp.float32)] * 2


def coarse_work(n):
    return [pltpu.VMEM((n * CC, CX, CY), jnp.float32)] * 2


def call(kernel, out_shape, in_specs, args, scratch=(), out_specs=None, **kw):
    if out_specs is None:
        out_specs = (VM,) * len(out_shape) if isinstance(out_shape, tuple) else VM
    return pl.pallas_call(
        kernel,
        out_shape=out_shape,
        in_specs=in_specs,
        out_specs=out_specs,
        scratch_shapes=list(scratch),
        compiler_params=PARAMS,
        **kw,
    )(*args)


def both(array, slabs):
    count = lax.axis_size("gz")
    out = []
    for edge in (1, 0):
        pairs = [(k * count + i, k * count + i + 1) for k in slabs for i in range(edge, count - 1, 2)]
        out.append(lax.ppermute(array, ("tm", "gz"), pairs + [(j, i) for i, j in pairs]))
    return out[0], out[1]


def handed(array, slabs, by=0, swap=()):
    count = lax.axis_size("gz")
    pairs = [(a * count + i, b * count + i + by) for a, b in slabs for i in range(count) if 0 <= i + by < count]
    for k in swap:
        for i in range(int(by == 1), count - 1, 2):
            pairs += [(k * count + i, k * count + i + 1), (k * count + i + 1, k * count + i)]
    return lax.ppermute(array, ("tm", "gz"), pairs)


def per_device(start_states):
    blocks = lax.axis_size("gz")
    slabs = lax.axis_size("tm")
    place = jnp.stack([lax.axis_index("gz"), lax.axis_index("tm")]).astype(jnp.int32)
    evens, odds = range(0, slabs, 2), range(1, slabs, 2)
    start_states = pltpu.with_memory_space_constraint(start_states, pltpu.HBM)
    own = call(prep_kernel, fine_shape, [HB], (start_states,), WHOLE)
    near = both(own, evens)
    word_shape = jax.ShapeDtypeStruct((8, CY), jnp.float32)
    word = handed(call(word_kernel, word_shape, [VM], (own,)), [(k, k + 1) for k in evens])
    own1, word = lax.optimization_barrier((own, word))
    near1 = both(own1, odds)
    fine = [SM] + [VM] * 3
    mid = call(functools.partial(fine_kernel, blocks, 0), fine_shape, fine, (place, own, *near), FINE_WORK)
    next0 = both(mid, evens)
    mid1 = call(
        functools.partial(fine_kernel, blocks, 1), fine_shape, fine + [HB], (place, own1, *near1, word), FINE_WORK
    )
    next1 = both(mid1, odds)
    old = call(
        functools.partial(coarse_kernel, blocks),
        coarse_shape,
        [SM] + [VM] * 5,
        (place, own, *near, *near1),
        coarse_work(3),
    )
    fine_end, jump, send = call(
        functools.partial(last_fine_kernel, blocks, 0),
        (fine_shape, coarse_shape, coarse_shape),
        [SM] + [VM] * 4,
        (place, mid, *next0, old),
        FINE_WORK,
    )
    fine_end, jump = call(
        functools.partial(last_fine_kernel, blocks, 1),
        (fine_shape, coarse_shape),
        [SM] + [VM] * 6,
        (place, mid1, *next1, old, fine_end, jump),
        FINE_WORK,
        input_output_aliases={5: 0, 6: 1},
    )
    firsts = range(0, slabs - 1, 2)
    pairs = [(k, k + 1) for k in firsts if k != 2]
    side = [handed(send, pairs, by, (2,) if by else ()) for by in (0, 1, -1)]
    wide_shape = jax.ShapeDtypeStruct((3 * CC, CX, CY), jnp.float32)
    picked, send, wide = call(
        functools.partial(first_sweep_kernel, blocks),
        (coarse_shape, coarse_shape, wide_shape),
        [SM] + [VM] * 5,
        (place, *side, jump, old),
        coarse_work(3),
    )

    def end_fine(part, *after):
        return call(
            functools.partial(last_fine_kernel, blocks, part),
            (fine_shape, coarse_shape),
            [SM] + [VM] * 6 + [HB] * len(after),
            (place, mid1, *next1, old, fine_end, jump, *after),
            FINE_WORK,
            input_output_aliases={5: 0, 6: 1},
        )

    fine_end, jump = end_fine(2, send)
    even = old
    for k in firsts[1:]:
        if k == 4:
            fine_end, jump = end_fine(3, send)
            rest = call(rest_kernel, half_shape, [VM] * 2, (fine_end, old))
        early = (rest,) if k == firsts[-1] else ()
        got = [handed(send, [(k - 1, k + 1)], by) for by in (2, -2, 1, -1, 0)]
        near = wide
        if k == 2:
            near, jump, *got = lax.optimization_barrier((wide, jump, *got))
            near = handed(near, [(2, 3)])
        if k == 2:
            even, state = call(
                functools.partial(even_sweep_kernel, blocks, k + 1),
                (coarse_shape, wide_shape),
                [SM] + [VM] * 6 + [HB] * len(early),
                (place, *got, even, *early),
                coarse_work(5),
            )
            picked, send = call(
                functools.partial(odd_sweep_kernel, blocks, k + 1),
                (coarse_shape,) * 2,
                [SM] + [VM] * 4,
                (place, state, near, jump, picked),
                coarse_work(3),
            )
        else:
            more = k != firsts[-1]
            picked, even, *rests = call(
                functools.partial(sweep_kernel, blocks, k + 1),
                (coarse_shape,) * (2 + more),
                [SM] + [VM] * 9 + [HB] * len(early),
                (place, *got, near, jump, picked, even, *early),
                coarse_work(1)[: 1 - more] + coarse_work(5),
            )
            send = rests[0] if more else None
    even = handed(even, [(k + 1, k) for k in firsts[1:]])
    return call(
        final_kernel,
        jax.ShapeDtypeStruct((1, CZ, NX, NY), jnp.float32),
        [SM] + [VM] * 3,
        (place, rest, picked, even),
        HALVES,
        HB,
    )


def solution(mesh):
    placed = (P("tm", "gz", None, None),)
    return jax.shard_map(
        per_device, mesh=mesh, in_specs=placed, out_specs=P("tm", "gz", None, None), check_vma=False
    )
```
